32 devices in a mesh: groups: 2 (over x), row: 16 (over z, y, core).
Axes of the slice: x: 2, y: 2, z: 4, core: 2. Of those that a mesh axis runs over, the one named last changes fastest.
Arguments:
- alignment_features: bfloat16 [512, 512, 256], P(('groups', 'row')), parts along dimension 0, may hold values from -6 to 6
- standardizer_gain: float32 [256], replicated, may hold values from 0.1 to 1.9
- standardizer_shift: float32 [256], replicated, may hold values from -3 to 3
- first_factor_kernel: bfloat16 [256, 32], replicated, may hold values from -0.375 to 0.375
- first_factor_shift: float32 [32], replicated, may hold values from -3 to 3
- second_factor_kernel: bfloat16 [256, 32], replicated, may hold values from -0.375 to 0.375
- second_factor_shift: float32 [32], replicated, may hold values from -3 to 3
- final_map_kernel: bfloat16 [1024, 128], replicated, may hold values from -0.75 to 0.75
- final_map_shift: float32 [128], replicated, may hold values from -3 to 3
Outputs:
- pair_update: bfloat16 [1024, 512, 128], P(('groups', 'row')), parts along dimension 0
The draws below stay inside these ranges and needn't reach their ends.
There are 2 independent parts, one for each index of `groups`. The reference program is written for one: setup_inputs(seed, part) draws one part's arguments, and reference() takes and returns one part's arrays. A program takes and returns all parts, laid end to end along the dimension named above; an argument that names none is the same for every part. Nothing has to cross between parts.
All inputs are finite; a program needn't handle non-finite values.
Results may differ from the reference program's by a relative error of at most 0.0055.
Values may be sent and summed in bfloat16 or wider, within the bound.
A program may use at most 128 MiB of HBM per device.

```python
import math
import jax
import jax.numpy as jnp
from jax import lax

FEATURE_DEPTH = 256
HIDDEN_WIDTH = 32
PAIR = 128
HOMOLOG_TOTAL = 256
AMINO_TOTAL = 512


def steps_of(rng, extent, shards, low, largest):
    def one(dim, parts):
        draws = jax.random.uniform(jax.random.fold_in(jax.random.fold_in(rng, 6), dim), (parts,), jnp.float32, low / len(shards), largest / len(shards))
        return jnp.repeat(jnp.exp(draws), extent[dim] // parts).reshape((-1,) + (1,) * (len(extent) - dim - 1))

    level = one(*shards[0])
    for cut in shards[1:]:
        level = level * one(*cut)
    return level


def scatter_about(stream_key, shape, scale, limit, cuts=(), dtype=jnp.bfloat16):
    values = scale * jax.random.normal(stream_key, shape, jnp.float32)
    if cuts:
        values = values * steps_of(stream_key, shape, cuts, -0.22, 0.18)
    return jnp.clip(values, -limit, limit).astype(dtype)


def setup_inputs(seed: int = 0, part: int = 0) -> dict:
    key_of = jax.random.split(jax.random.key(seed), 10)
    part_keys = jax.random.split(jax.random.fold_in(key_of[9], part), 10)
    return {
        "alignment_features": scatter_about(part_keys[0], (HOMOLOG_TOTAL, AMINO_TOTAL, FEATURE_DEPTH), 1.0, 6.0, ((0, 16),)),
        "standardizer_gain": jnp.clip(1.0 + 0.18 * jax.random.normal(key_of[1], (FEATURE_DEPTH,), jnp.float32), 0.1, 1.9),
        "standardizer_shift": scatter_about(key_of[2], (FEATURE_DEPTH,), 0.3, 3.0, (), jnp.float32),
        "first_factor_kernel": scatter_about(key_of[3], (FEATURE_DEPTH, HIDDEN_WIDTH), FEATURE_DEPTH ** -0.5, 0.375),
        "first_factor_shift": scatter_about(key_of[4], (HIDDEN_WIDTH,), 0.25, 3.0, (), jnp.float32),
        "second_factor_kernel": scatter_about(key_of[5], (FEATURE_DEPTH, HIDDEN_WIDTH), FEATURE_DEPTH ** -0.5, 0.375),
        "second_factor_shift": scatter_about(key_of[6], (HIDDEN_WIDTH,), 0.25, 3.0, (), jnp.float32),
        "final_map_kernel": scatter_about(key_of[7], (HIDDEN_WIDTH * HIDDEN_WIDTH, PAIR), (2 * HIDDEN_WIDTH) ** -0.5, 0.75),
        "final_map_shift": scatter_about(key_of[8], (PAIR,), 0.3, 3.0, (), jnp.float32),
    }


def standardize_then_map(alignment_features, standardizer_gain, standardizer_shift, kernel_array, window_start):
    incoming_features = alignment_features.astype(jnp.float32)
    center = incoming_features - lax.optimization_barrier(jnp.mean(incoming_features, axis=-1, keepdims=True))
    spread = lax.optimization_barrier(jnp.mean(center * center, axis=-1, keepdims=True))
    normed = (center * lax.rsqrt(spread + 1e-05) * standardizer_gain + standardizer_shift).astype(jnp.bfloat16)
    normed = lax.optimization_barrier(normed).astype(jnp.float32)
    result = jnp.einsum('src,ck->rsk', normed, kernel_array.astype(jnp.float32)) + window_start
    result = lax.optimization_barrier(result.astype(jnp.bfloat16))
    return result.astype(jnp.float32)

def reference(alignment_features, standardizer_gain, standardizer_shift, first_factor_kernel, first_factor_shift, second_factor_kernel, second_factor_shift, final_map_kernel, final_map_shift):
    first_factor_features = standardize_then_map(alignment_features, standardizer_gain, standardizer_shift, first_factor_kernel, first_factor_shift)
    second_factor_features = standardize_then_map(alignment_features, standardizer_gain, standardizer_shift, second_factor_kernel, second_factor_shift)
    blocksize = math.gcd(AMINO_TOTAL, 32)
    left_blocks = first_factor_features.reshape(AMINO_TOTAL // blocksize, blocksize, HOMOLOG_TOTAL, HIDDEN_WIDTH)
    out_weight = final_map_kernel.astype(jnp.float32)

    def one_block(left_rows):
        outer = jnp.einsum('isc,jsd->ijcd', left_rows, second_factor_features) / HOMOLOG_TOTAL
        outer = lax.optimization_barrier(outer.astype(jnp.bfloat16)).astype(jnp.float32)
        flat = outer.reshape(blocksize, AMINO_TOTAL, HIDDEN_WIDTH * HIDDEN_WIDTH)
        return (jnp.einsum('ijk,kp->ijp', flat, out_weight) + final_map_shift).astype(jnp.bfloat16)
    blocks = lax.map(one_block, left_blocks)
    return blocks.reshape(AMINO_TOTAL, AMINO_TOTAL, PAIR)
```

```python
import functools

import jax
import jax.numpy as jnp
from jax import lax
from jax.experimental import pallas as pl
from jax.experimental.pallas import tpu as pltpu
from jax.sharding import PartitionSpec as P

LANES = 128
SUBLANES = 8


def largest_divisor(total, limit):
    return max((factor for factor in range(1, min(total, limit) + 1) if total % factor == 0))


def project_flat(
    block,
    standardizer_gain,
    standardizer_shift,
    first_factor_kernel,
    first_factor_shift,
    second_factor_kernel,
    second_factor_shift,
):
    incoming_features = block.astype(jnp.float32)
    center = incoming_features - jnp.mean(incoming_features, axis=-1, keepdims=True)
    spread = jnp.mean(center * center, axis=-1, keepdims=True)
    normed = (center * lax.rsqrt(spread + 1e-05) * standardizer_gain + standardizer_shift).astype(
        jnp.bfloat16
    )
    lines, residues = (normed.shape[0], normed.shape[1])
    first_mapped = jnp.einsum(
        "src,ck->srk", normed, first_factor_kernel, preferred_element_type=jnp.float32
    )
    second_mapped = jnp.einsum(
        "src,ck->srk", normed, second_factor_kernel, preferred_element_type=jnp.float32
    )
    first_flat = (first_mapped + first_factor_shift).astype(jnp.bfloat16).reshape(lines, -1)
    second_flat = (second_mapped + second_factor_shift).astype(jnp.bfloat16).reshape(lines, -1)
    return (first_flat, second_flat)


def pair_rows(left_flat, right_flat, width, final_map_kernel, final_map_shift):
    count = left_flat.shape[0]
    rows = left_flat.shape[1] // width
    cols = right_flat.shape[1] // width
    pair_width = final_map_kernel.shape[1]
    row_step = largest_divisor(rows, max(1, 2048 // cols))
    kernel_grid = final_map_kernel.reshape(width, width, pair_width)

    def one_block(index):
        left_part = lax.dynamic_slice_in_dim(
            left_flat, index * (row_step * width), row_step * width, 1
        )
        outer = lax.dot_general(
            left_part, right_flat, (((0,), (0,)), ((), ())), preferred_element_type=jnp.float32
        )
        outer = (outer / count).astype(jnp.bfloat16).reshape(row_step, width, cols, width)
        mapped = jnp.einsum("icjd,cdp->ijp", outer, kernel_grid, preferred_element_type=jnp.float32)
        return (mapped + final_map_shift).astype(jnp.bfloat16)

    blocks = lax.map(one_block, jnp.arange(rows // row_step, dtype=jnp.int32))
    return blocks.reshape(rows, cols, pair_width)


def project_kernel(
    features,
    gain,
    offset,
    first_spread,
    first_bias,
    second_t,
    second_bias,
    left_out,
    right_out,
    first_rows,
    second_rows,
):
    lines, span, depth = features.shape
    width = second_t.shape[0]
    fold = LANES // width
    owners = span // (fold * SUBLANES)
    incoming = features[...].astype(jnp.float32).reshape(lines * span, depth)
    center = incoming - jnp.mean(incoming, axis=-1, keepdims=True)
    spread = jnp.mean(center * center, axis=-1, keepdims=True)
    normed = center * lax.rsqrt(spread + 1e-05) * gain[...] + offset[...]
    split = normed.reshape(lines * owners, fold, SUBLANES, depth)
    folded = jnp.concatenate(
        [split[:, m].reshape(lines * owners * SUBLANES, depth).astype(jnp.bfloat16) for m in range(fold)],
        axis=1,
    )
    first_rows[...] = (
        jnp.dot(folded, first_spread[...], preferred_element_type=jnp.float32) + first_bias[...]
    )
    flat = normed.astype(jnp.bfloat16)
    for s in range(lines):
        second_rows[s * width : (s + 1) * width, :] = (
            lax.dot_general(
                second_t[...],
                flat[s * span : (s + 1) * span],
                (((1,), (1,)), ((), ())),
                preferred_element_type=jnp.float32,
            )
            + second_bias[...]
        )
    per_line = owners * SUBLANES
    for q in range(per_line):
        left_out[:, q * LANES : (q + 1) * LANES] = first_rows[
            pl.ds(q, lines, stride=per_line), :
        ].astype(jnp.bfloat16)
    for d in range(width):
        right_out[:, d * span : (d + 1) * span] = second_rows[
            pl.ds(d, lines, stride=width), :
        ].astype(jnp.bfloat16)


def project(features, gain, offset, first_kernel, first_bias, second_kernel, second_bias):
    lines, residues, depth = features.shape
    width = first_kernel.shape[1]
    fold = LANES // width
    chunks = residues // LANES
    first_spread = jnp.einsum("mn,ck->mcnk", jnp.eye(fold, dtype=first_kernel.dtype), first_kernel)
    first_spread = first_spread.reshape(fold * depth, LANES)
    whole = pl.BlockSpec(memory_space=pltpu.VMEM)
    return pl.pallas_call(
        project_kernel,
        grid=(chunks,),
        in_specs=[pl.BlockSpec((lines, LANES, depth), lambda k: (0, k, 0))] + [whole] * 6,
        out_specs=[
            pl.BlockSpec((lines, LANES * width), lambda k: (0, k)),
            pl.BlockSpec((lines, LANES * width), lambda k: (0, k)),
        ],
        out_shape=[jax.ShapeDtypeStruct((lines, residues * width), jnp.bfloat16)] * 2,
        scratch_shapes=[
            pltpu.VMEM((lines * LANES // fold, LANES), jnp.float32),
            pltpu.VMEM((lines * width, LANES), jnp.float32),
        ],
        compiler_params=pltpu.CompilerParams(vmem_limit_bytes=48 * 1024 * 1024),
    )(
        features,
        gain.reshape(1, depth),
        offset.reshape(1, depth),
        first_spread,
        jnp.tile(first_bias, fold).reshape(1, LANES),
        second_kernel.T,
        second_bias.reshape(width, 1),
    )


def pair_kernel(left_t, right, map_t, map_bias, out, outer):
    rows, span, pair_width = out.shape
    count = right.shape[0]
    width = right.shape[1] // span
    fold = LANES // width

    @pl.loop(0, width // 2)
    def _(step):
        part = jnp.dot(
            left_t[...],
            right[:, pl.ds(pl.multiple_of(step * (2 * span), 2 * span), 2 * span)],
            preferred_element_type=jnp.float32,
        )
        part = part.astype(jnp.bfloat16).reshape(rows // 2, 2, width, 2 * span)
        for half in range(2):
            place = pl.ds(pl.multiple_of(step * (2 * width) + half * width, width), width)
            for side in range(2):
                outer[:, place, side * span : (side + 1) * span] = part[
                    :, side, :, half * span : (half + 1) * span
                ]

    @pl.loop(0, rows // 2)
    def _(pair):
        mapped = jnp.dot(map_t[...], outer[pair], preferred_element_type=jnp.float32)
        mapped = mapped * (1.0 / count) + map_bias[...]
        for side in range(2):
            block = 2 * pair + side
            row = (block % fold) * SUBLANES + block // fold
            out[row] = mapped[:, side * span : (side + 1) * span].T.astype(jnp.bfloat16)


def pair_update(left_t, right, final_map_kernel, final_map_bias, rows):
    count = right.shape[0]
    pair_width = final_map_kernel.shape[1]
    width = left_t.shape[0] // rows
    cols = right.shape[1] // width
    map_t = final_map_kernel.reshape(width, width, pair_width).transpose(2, 1, 0)
    whole = pl.BlockSpec(memory_space=pltpu.VMEM)
    return pl.pallas_call(
        pair_kernel,
        grid=(cols // LANES,),
        in_specs=[
            whole,
            pl.BlockSpec((count, LANES * width), lambda k: (0, k)),
            whole,
            whole,
        ],
        out_specs=pl.BlockSpec((rows, LANES, pair_width), lambda k: (0, k, 0)),
        out_shape=jax.ShapeDtypeStruct((rows, cols, pair_width), jnp.bfloat16),
        scratch_shapes=[pltpu.VMEM((rows // 2, width * width, 2 * LANES), jnp.bfloat16)],
        compiler_params=pltpu.CompilerParams(vmem_limit_bytes=48 * 1024 * 1024),
    )(left_t, right, map_t.reshape(pair_width, width * width), final_map_bias.reshape(pair_width, 1))


def body(
    alignment_features,
    standardizer_gain,
    standardizer_shift,
    first_factor_kernel,
    first_factor_shift,
    second_factor_kernel,
    second_factor_shift,
    final_map_kernel,
    final_map_shift,
):
    left, right = project(
        alignment_features,
        standardizer_gain,
        standardizer_shift,
        first_factor_kernel,
        first_factor_shift,
        second_factor_kernel,
        second_factor_shift,
    )
    rows = alignment_features.shape[1] // lax.axis_size("row")
    left_t = lax.all_to_all(left, "row", split_axis=1, concat_axis=0, tiled=True).T
    return pair_update(
        left_t,
        lax.all_gather(right, "row", axis=0, tiled=True),
        final_map_kernel,
        final_map_shift,
        rows,
    )


def plain_body(
    alignment_features,
    standardizer_gain,
    standardizer_shift,
    first_factor_kernel,
    first_factor_shift,
    second_factor_kernel,
    second_factor_shift,
    final_map_kernel,
    final_map_shift,
):
    width = first_factor_kernel.shape[1]
    arrived_lines = lax.all_to_all(
        alignment_features, "row", split_axis=1, concat_axis=0, tiled=True
    )
    left_flat, right_flat = project_flat(
        arrived_lines,
        standardizer_gain,
        standardizer_shift,
        first_factor_kernel,
        first_factor_shift,
        second_factor_kernel,
        second_factor_shift,
    )
    return pair_rows(
        left_flat,
        lax.all_gather(right_flat, "row", axis=1, tiled=True),
        width,
        final_map_kernel,
        final_map_shift,
    )


def solution(mesh):
    ways = mesh.shape["row"]
    groups = mesh.shape["groups"]

    def update(alignment_features, *parameters):
        total, residues, depth = alignment_features.shape
        width = parameters[2].shape[1]
        lines = total // (groups * ways)
        count = lines * ways
        fits = (
            ways == 16
            and lines % 16 == 0
            and count & (count - 1) == 0
            and width == 32
            and residues == 32 * ways
            and depth % LANES == 0
            and parameters[6].shape[1] == LANES
        )
        return jax.shard_map(
            body if fits else plain_body,
            mesh=mesh,
            in_specs=(P(("groups", "row"), None, None),) + (P(),) * len(parameters),
            out_specs=P(("groups", "row"), None, None),
            check_vma=False,
        )(alignment_features, *parameters)

    return update
```

```python
import functools

import jax
import jax.numpy as jnp
from jax import lax
from jax.experimental import pallas as pl
from jax.experimental.pallas import tpu as pltpu
from jax.sharding import PartitionSpec as P

LANES = 128
SUBLANES = 8


def largest_divisor(total, limit):
    return max((factor for factor in range(1, min(total, limit) + 1) if total % factor == 0))


def project_flat(
    block,
    standardizer_gain,
    standardizer_shift,
    first_factor_kernel,
    first_factor_shift,
    second_factor_kernel,
    second_factor_shift,
):
    incoming_features = block.astype(jnp.float32)
    center = incoming_features - jnp.mean(incoming_features, axis=-1, keepdims=True)
    spread = jnp.mean(center * center, axis=-1, keepdims=True)
    normed = (center * lax.rsqrt(spread + 1e-05) * standardizer_gain + standardizer_shift).astype(
        jnp.bfloat16
    )
    lines, residues = (normed.shape[0], normed.shape[1])
    first_mapped = jnp.einsum(
        "src,ck->srk", normed, first_factor_kernel, preferred_element_type=jnp.float32
    )
    second_mapped = jnp.einsum(
        "src,ck->srk", normed, second_factor_kernel, preferred_element_type=jnp.float32
    )
    first_flat = (first_mapped + first_factor_shift).astype(jnp.bfloat16).reshape(lines, -1)
    second_flat = (second_mapped + second_factor_shift).astype(jnp.bfloat16).reshape(lines, -1)
    return (first_flat, second_flat)


def pair_rows(left_flat, right_flat, width, final_map_kernel, final_map_shift):
    count = left_flat.shape[0]
    rows = left_flat.shape[1] // width
    cols = right_flat.shape[1] // width
    pair_width = final_map_kernel.shape[1]
    row_step = largest_divisor(rows, max(1, 2048 // cols))
    kernel_grid = final_map_kernel.reshape(width, width, pair_width)

    def one_block(index):
        left_part = lax.dynamic_slice_in_dim(
            left_flat, index * (row_step * width), row_step * width, 1
        )
        outer = lax.dot_general(
            left_part, right_flat, (((0,), (0,)), ((), ())), preferred_element_type=jnp.float32
        )
        outer = (outer / count).astype(jnp.bfloat16).reshape(row_step, width, cols, width)
        mapped = jnp.einsum("icjd,cdp->ijp", outer, kernel_grid, preferred_element_type=jnp.float32)
        return (mapped + final_map_shift).astype(jnp.bfloat16)

    blocks = lax.map(one_block, jnp.arange(rows // row_step, dtype=jnp.int32))
    return blocks.reshape(rows, cols, pair_width)


def project_kernel(
    features,
    gain,
    offset,
    first_spread,
    first_bias,
    second_t,
    second_bias,
    left_out,
    right_out,
    first_rows,
    second_rows,
):
    lines, span, depth = features.shape
    width = second_t.shape[0]
    fold = LANES // width
    owners = span // (fold * SUBLANES)
    incoming = features[...].astype(jnp.float32).reshape(lines * span, depth)
    center = incoming - jnp.mean(incoming, axis=-1, keepdims=True)
    spread = jnp.mean(center * center, axis=-1, keepdims=True)
    normed = center * lax.rsqrt(spread + 1e-05) * gain[...] + offset[...]
    split = normed.reshape(lines * owners, fold, SUBLANES, depth)
    folded = jnp.concatenate(
        [split[:, m].reshape(lines * owners * SUBLANES, depth).astype(jnp.bfloat16) for m in range(fold)],
        axis=1,
    )
    first_rows[...] = (
        jnp.dot(folded, first_spread[...], preferred_element_type=jnp.float32) + first_bias[...]
    )
    flat = normed.astype(jnp.bfloat16)
    for s in range(lines):
        second_rows[s * width : (s + 1) * width, :] = (
            lax.dot_general(
                second_t[...],
                flat[s * span : (s + 1) * span],
                (((1,), (1,)), ((), ())),
                preferred_element_type=jnp.float32,
            )
            + second_bias[...]
        )
    per_line = owners * SUBLANES
    for q in range(per_line):
        left_out[:, q * LANES : (q + 1) * LANES] = first_rows[
            pl.ds(q, lines, stride=per_line), :
        ].astype(jnp.bfloat16)
    for d in range(width):
        right_out[:, d * span : (d + 1) * span] = second_rows[
            pl.ds(d, lines, stride=width), :
        ].astype(jnp.bfloat16)


def project(features, gain, offset, first_kernel, first_bias, second_kernel, second_bias):
    lines, residues, depth = features.shape
    width = first_kernel.shape[1]
    fold = LANES // width
    chunks = residues // LANES
    first_spread = jnp.einsum("mn,ck->mcnk", jnp.eye(fold, dtype=first_kernel.dtype), first_kernel)
    first_spread = first_spread.reshape(fold * depth, LANES)
    whole = pl.BlockSpec(memory_space=pltpu.VMEM)
    return pl.pallas_call(
        project_kernel,
        grid=(chunks,),
        in_specs=[pl.BlockSpec((lines, LANES, depth), lambda k: (0, k, 0))] + [whole] * 6,
        out_specs=[
            pl.BlockSpec((lines, LANES * width), lambda k: (0, k)),
            pl.BlockSpec((lines, LANES * width), lambda k: (0, k)),
        ],
        out_shape=[jax.ShapeDtypeStruct((lines, residues * width), jnp.bfloat16)] * 2,
        scratch_shapes=[
            pltpu.VMEM((lines * LANES // fold, LANES), jnp.float32),
            pltpu.VMEM((lines * width, LANES), jnp.float32),
        ],
        compiler_params=pltpu.CompilerParams(vmem_limit_bytes=48 * 1024 * 1024),
    )(
        features,
        gain.reshape(1, depth),
        offset.reshape(1, depth),
        first_spread,
        jnp.tile(first_bias, fold).reshape(1, LANES),
        second_kernel.T,
        second_bias.reshape(width, 1),
    )


MESH = pl.DeviceIdType.MESH


def fused_kernel(
    ways,
    left_in,
    right_in,
    map_t,
    map_bias,
    out,
    held,
    left_held,
    left_t,
    outer,
    left_send,
    left_recv,
    ring_send,
    ring_recv,
    share_send,
    share_recv,
):
    chunks, count, chunk_lanes = held.shape
    lines = right_in.shape[0]
    left_lanes = left_held.shape[1]
    rows = out.shape[0]
    span = LANES
    width = chunk_lanes // span
    fold = LANES // width
    chips = ways // 2
    side_chips = chips // 2
    half_lanes = chunk_lanes // 2
    far = chips // 2

    me = lax.axis_index("row")
    core = lax.rem(me, 2)
    chip = me // 2
    level = chip // 2
    flank = lax.rem(chip, 2)
    place = level + flank * (chips - 1 - 2 * level)

    def device_at(position, kernel):
        turned = position // side_chips
        return 2 * (2 * position + turned * (2 * chips - 1 - 4 * position)) + kernel

    onward = (
        device_at(lax.rem(place + 1, chips), core),
        device_at(lax.rem(place + chips - 1, chips), core),
    )
    partner = me + 1 - 2 * core

    def origin(direction, hop):
        shift = chips - hop if direction == 0 else hop
        return lax.rem(place + shift, chips)

    def lines_of(device):
        return pl.ds(pl.multiple_of(device * lines, lines), lines)

    def ring(k, direction, half, hop, distance):
        ref = held.at[
            k,
            lines_of(device_at(origin(direction, distance), core)),
            pl.ds(half * half_lanes, half_lanes),
        ]
        return pltpu.make_async_remote_copy(
            src_ref=ref,
            dst_ref=ref,
            send_sem=ring_send.at[k, direction, half, hop - 1],
            recv_sem=ring_recv.at[k, direction, half, hop - 1],
            device_id={"row": onward[direction]},
            device_id_type=MESH,
        )

    def ring_start(k, direction, half, hop):
        ring(k, direction, half, hop, hop - 1).start()

    def ring_wait(k, direction, half, hop):
        ring(k, direction, half, hop, hop).wait_recv()

    def share(k, slot, kernel):
        direction = 0 if slot <= far else 1
        hop = slot if slot <= far else slot - far
        ref = held.at[k, lines_of(device_at(origin(direction, hop), kernel))]
        return pltpu.make_async_remote_copy(
            src_ref=ref,
            dst_ref=ref,
            send_sem=share_send.at[k, slot],
            recv_sem=share_recv.at[k, slot],
            device_id={"row": partner},
            device_id_type=MESH,
        )

    def begin(k):
        for half in range(2):
            for direction in range(2):
                ring_start(k, direction, half, 1)
        share(k, 0, core).start()

    def left_copy(step, target, source):
        return pltpu.make_async_remote_copy(
            src_ref=left_in.at[:, pl.ds(pl.multiple_of(target * left_lanes, left_lanes), left_lanes)],
            dst_ref=left_held.at[lines_of(source)],
            send_sem=left_send.at[step - 1],
            recv_sem=left_recv.at[step - 1],
            device_id={"row": target},
            device_id_type=MESH,
        )

    def outer_steps(k, first, last):
        @pl.loop(first, last)
        def _(step):
            part = jnp.dot(
                left_t[...],
                held[k, :, pl.ds(pl.multiple_of(step * (2 * span), 2 * span), 2 * span)],
                preferred_element_type=jnp.float32,
            )
            part = part.astype(jnp.bfloat16).reshape(rows // 2, 2, width, 2 * span)
            for half in range(2):
                spot = pl.ds(pl.multiple_of(step * (2 * width) + half * width, width), width)
                for side in range(2):
                    outer[:, spot, side * span : (side + 1) * span] = part[
                        :, side, :, half * span : (half + 1) * span
                    ]

    def map_steps(k, first, last):
        @pl.loop(first, last)
        def _(pair):
            mapped = jnp.dot(map_t[...], outer[pair], preferred_element_type=jnp.float32)
            mapped = mapped * (1.0 / count) + map_bias[...]
            for side in range(2):
                block = 2 * pair + side
                row = lax.rem(block, fold) * SUBLANES + block // fold
                out[row, pl.ds(pl.multiple_of(k * span, span), span), :] = mapped[
                    :, side * span : (side + 1) * span
                ].T.astype(jnp.bfloat16)

    barrier = pltpu.get_barrier_semaphore()

    @pl.loop(1, ways)
    def _(step):
        pl.semaphore_signal(
            barrier, inc=1, device_id={"row": lax.rem(me + step, ways)}, device_id_type=MESH
        )

    for k in range(chunks):
        held[k, lines_of(me), :] = right_in[:, k * chunk_lanes : (k + 1) * chunk_lanes]
    pl.semaphore_wait(barrier, ways - 1)

    @pl.loop(1, ways)
    def _(step):
        left_copy(step, lax.rem(me + step, ways), me).start()

    begin(0)
    left_held[lines_of(me), :] = left_in[
        :, pl.ds(pl.multiple_of(me * left_lanes, left_lanes), left_lanes)
    ]

    quarter = width // 8
    third = rows // 2 // 4

    @pl.loop(0, chunks)
    def _(k):
        def beside(work, number, size):
            @pl.when(k > 0)
            def _():
                work(k - 1, number * size, (number + 1) * size)

        for hop in range(1, far):
            for half in range(2):
                for direction in range(2):
                    ring_wait(k, direction, half, hop)
                    if hop + 1 < far or half == direction:
                        ring_start(k, direction, half, hop + 1)
                if half == 1:
                    share(k, hop, core).start()
                    share(k, far + hop, core).start()
                    if hop == 1:

                        @pl.when(k + 1 < chunks)
                        def _():
                            begin(k + 1)

                number = 2 * (hop - 1) + half
                if number < 4:
                    beside(outer_steps, number, quarter)
                else:
                    beside(map_steps, number - 4, third)
        ring_wait(k, 0, 0, far)
        ring_wait(k, 1, 1, far)
        share(k, far, core).start()
        beside(map_steps, 2, third)
        beside(map_steps, 3, third)

        for slot in range(chips):
            share(k, slot, 1 - core).wait_recv()

        @pl.when(k == 0)
        def _():
            @pl.loop(1, ways)
            def _(step):
                source = lax.rem(me + ways - step, ways)
                left_copy(step, lax.rem(me + step, ways), source).wait_recv()

            for at in range(0, left_lanes, 2 * LANES):
                left_t[at : at + 2 * LANES, :] = (
                    left_held[:, at : at + 2 * LANES].astype(jnp.float32).T.astype(jnp.bfloat16)
                )

    outer_steps(chunks - 1, 0, width // 2)
    map_steps(chunks - 1, 0, rows // 2)

    @pl.loop(1, ways)
    def _(step):
        left_copy(step, lax.rem(me + step, ways), me).wait_send()

    @pl.loop(0, chunks)
    def _(k):
        for direction in range(2):
            for half in range(2):
                for hop in range(1, far + 1):
                    if hop < far or half == direction:
                        ring(k, direction, half, hop, hop - 1).wait_send()
        for slot in range(chips):
            share(k, slot, core).wait_send()


def exchange_and_pair(left, right, final_map_kernel, final_map_bias, rows, ways):
    lines = right.shape[0]
    count = lines * ways
    pair_width = final_map_kernel.shape[1]
    cols = rows * ways
    width = right.shape[1] // cols
    chunks = cols // LANES
    chips = ways // 2
    map_t = final_map_kernel.reshape(width, width, pair_width).transpose(2, 1, 0)
    whole = pl.BlockSpec(memory_space=pltpu.VMEM)
    return pl.pallas_call(
        functools.partial(fused_kernel, ways),
        in_specs=[whole] * 4,
        out_specs=whole,
        out_shape=jax.ShapeDtypeStruct((rows, cols, pair_width), jnp.bfloat16),
        scratch_shapes=[
            pltpu.VMEM((chunks, count, LANES * width), jnp.bfloat16),
            pltpu.VMEM((count, rows * width), jnp.bfloat16),
            pltpu.VMEM((rows * width, count), jnp.bfloat16),
            pltpu.VMEM((rows // 2, width * width, 2 * LANES), jnp.bfloat16),
            pltpu.SemaphoreType.DMA((ways - 1,)),
            pltpu.SemaphoreType.DMA((ways - 1,)),
            pltpu.SemaphoreType.DMA((chunks, 2, 2, chips // 2)),
            pltpu.SemaphoreType.DMA((chunks, 2, 2, chips // 2)),
            pltpu.SemaphoreType.DMA((chunks, chips)),
            pltpu.SemaphoreType.DMA((chunks, chips)),
        ],
        compiler_params=pltpu.CompilerParams(
            collective_id=0, has_side_effects=True, vmem_limit_bytes=48 * 1024 * 1024
        ),
    )(
        left,
        right,
        map_t.reshape(pair_width, width * width),
        final_map_bias.reshape(pair_width, 1),
    )


def body(
    alignment_features,
    standardizer_gain,
    standardizer_shift,
    first_factor_kernel,
    first_factor_shift,
    second_factor_kernel,
    second_factor_shift,
    final_map_kernel,
    final_map_shift,
):
    left, right = project(
        alignment_features,
        standardizer_gain,
        standardizer_shift,
        first_factor_kernel,
        first_factor_shift,
        second_factor_kernel,
        second_factor_shift,
    )
    ways = lax.axis_size("row")
    rows = alignment_features.shape[1] // ways
    return exchange_and_pair(left, right, final_map_kernel, final_map_shift, rows, ways)


def plain_body(
    alignment_features,
    standardizer_gain,
    standardizer_shift,
    first_factor_kernel,
    first_factor_shift,
    second_factor_kernel,
    second_factor_shift,
    final_map_kernel,
    final_map_shift,
):
    width = first_factor_kernel.shape[1]
    arrived_lines = lax.all_to_all(
        alignment_features, "row", split_axis=1, concat_axis=0, tiled=True
    )
    left_flat, right_flat = project_flat(
        arrived_lines,
        standardizer_gain,
        standardizer_shift,
        first_factor_kernel,
        first_factor_shift,
        second_factor_kernel,
        second_factor_shift,
    )
    return pair_rows(
        left_flat,
        lax.all_gather(right_flat, "row", axis=1, tiled=True),
        width,
        final_map_kernel,
        final_map_shift,
    )


def solution(mesh):
    ways = mesh.shape["row"]
    groups = mesh.shape["groups"]

    def update(alignment_features, *parameters):
        total, residues, depth = alignment_features.shape
        width = parameters[2].shape[1]
        lines = total // (groups * ways)
        count = lines * ways
        fits = (
            ways == 16
            and lines % 16 == 0
            and count & (count - 1) == 0
            and width == 32
            and residues == 32 * ways
            and depth % LANES == 0
            and parameters[6].shape[1] == LANES
        )
        return jax.shard_map(
            body if fits else plain_body,
            mesh=mesh,
            in_specs=(P(("groups", "row"), None, None),) + (P(),) * len(parameters),
            out_specs=P(("groups", "row"), None, None),
            check_vma=False,
        )(alignment_features, *parameters)

    return update
```

```python
import functools

import jax
import jax.numpy as jnp
from jax import lax
from jax.experimental import pallas as pl
from jax.experimental.pallas import tpu as pltpu
from jax.sharding import PartitionSpec as P

LANES = 128
SUBLANES = 8


def largest_divisor(total, limit):
    return max((factor for factor in range(1, min(total, limit) + 1) if total % factor == 0))


def project_flat(
    block,
    standardizer_gain,
    standardizer_shift,
    first_factor_kernel,
    first_factor_shift,
    second_factor_kernel,
    second_factor_shift,
):
    incoming_features = block.astype(jnp.float32)
    center = incoming_features - jnp.mean(incoming_features, axis=-1, keepdims=True)
    spread = jnp.mean(center * center, axis=-1, keepdims=True)
    normed = (center * lax.rsqrt(spread + 1e-05) * standardizer_gain + standardizer_shift).astype(
        jnp.bfloat16
    )
    lines, residues = (normed.shape[0], normed.shape[1])
    first_mapped = jnp.einsum(
        "src,ck->srk", normed, first_factor_kernel, preferred_element_type=jnp.float32
    )
    second_mapped = jnp.einsum(
        "src,ck->srk", normed, second_factor_kernel, preferred_element_type=jnp.float32
    )
    first_flat = (first_mapped + first_factor_shift).astype(jnp.bfloat16).reshape(lines, -1)
    second_flat = (second_mapped + second_factor_shift).astype(jnp.bfloat16).reshape(lines, -1)
    return (first_flat, second_flat)


def pair_rows(left_flat, right_flat, width, final_map_kernel, final_map_shift):
    count = left_flat.shape[0]
    rows = left_flat.shape[1] // width
    cols = right_flat.shape[1] // width
    pair_width = final_map_kernel.shape[1]
    row_step = largest_divisor(rows, max(1, 2048 // cols))
    kernel_grid = final_map_kernel.reshape(width, width, pair_width)

    def one_block(index):
        left_part = lax.dynamic_slice_in_dim(
            left_flat, index * (row_step * width), row_step * width, 1
        )
        outer = lax.dot_general(
            left_part, right_flat, (((0,), (0,)), ((), ())), preferred_element_type=jnp.float32
        )
        outer = (outer / count).astype(jnp.bfloat16).reshape(row_step, width, cols, width)
        mapped = jnp.einsum("icjd,cdp->ijp", outer, kernel_grid, preferred_element_type=jnp.float32)
        return (mapped + final_map_shift).astype(jnp.bfloat16)

    blocks = lax.map(one_block, jnp.arange(rows // row_step, dtype=jnp.int32))
    return blocks.reshape(rows, cols, pair_width)


def project_kernel(
    features,
    gain,
    offset,
    first_t,
    first_bias,
    second_t,
    second_bias,
    left_out,
    right_out,
    first_spread,
    first_rows,
    second_rows,
):
    lines, span, depth = features.shape
    width = second_t.shape[0]
    fold = LANES // width
    owners = span // (fold * SUBLANES)

    @pl.when(pl.program_id(0) == 0)
    def _():
        first_spread[...] = jnp.zeros_like(first_spread)
        for m in range(fold):
            first_spread[m * width : (m + 1) * width, m * depth : (m + 1) * depth] = first_t[...]

    incoming = features[...].astype(jnp.float32).reshape(lines * span, depth)
    center = incoming - jnp.mean(incoming, axis=-1, keepdims=True)
    spread = jnp.mean(center * center, axis=-1, keepdims=True)
    normed = center * lax.rsqrt(spread + 1e-05) * gain[...] + offset[...]
    split = normed.reshape(lines * owners, fold, SUBLANES, depth)
    folded = jnp.concatenate(
        [split[:, m].reshape(lines * owners * SUBLANES, depth).astype(jnp.bfloat16) for m in range(fold)],
        axis=1,
    )
    first_rows[...] = (
        lax.dot_general(
            folded, first_spread[...], (((1,), (1,)), ((), ())), preferred_element_type=jnp.float32
        )
        + jnp.concatenate([first_bias[...]] * fold, axis=1)
    )
    flat = normed.astype(jnp.bfloat16)
    for s in range(lines):
        second_rows[s * width : (s + 1) * width, :] = lax.dot_general(
            second_t[...],
            flat[s * span : (s + 1) * span],
            (((1,), (1,)), ((), ())),
            preferred_element_type=jnp.float32,
        )
    per_line = owners * SUBLANES
    for q in range(per_line):
        left_out[:, q * LANES : (q + 1) * LANES] = first_rows[
            pl.ds(q, lines, stride=per_line), :
        ].astype(jnp.bfloat16)
    for d in range(width):
        right_out[:, d * span : (d + 1) * span] = (
            second_rows[pl.ds(d, lines, stride=width), :] + second_bias[d]
        ).astype(jnp.bfloat16)


def project(features, gain, offset, first_kernel, first_bias, second_kernel, second_bias):
    lines, residues, depth = features.shape
    width = first_kernel.shape[1]
    fold = LANES // width
    chunks = residues // LANES
    whole = pl.BlockSpec(memory_space=pltpu.VMEM)
    return pl.pallas_call(
        project_kernel,
        grid=(chunks,),
        in_specs=[pl.BlockSpec((lines, LANES, depth), lambda k: (0, k, 0))]
        + [whole] * 5
        + [pl.BlockSpec(memory_space=pltpu.SMEM)],
        out_specs=[
            pl.BlockSpec((lines, LANES * width), lambda k: (0, k)),
            pl.BlockSpec((lines, LANES * width), lambda k: (0, k)),
        ],
        out_shape=[jax.ShapeDtypeStruct((lines, residues * width), jnp.bfloat16)] * 2,
        scratch_shapes=[
            pltpu.VMEM((LANES, fold * depth), jnp.bfloat16),
            pltpu.VMEM((lines * LANES // fold, LANES), jnp.float32),
            pltpu.VMEM((lines * width, LANES), jnp.float32),
        ],
        compiler_params=pltpu.CompilerParams(vmem_limit_bytes=58 * 1024 * 1024),
    )(
        features,
        gain.reshape(1, depth),
        offset.reshape(1, depth),
        first_kernel.T,
        first_bias.reshape(1, width),
        second_kernel.T,
        second_bias,
    )


MESH = pl.DeviceIdType.MESH


def fused_kernel(
    ways,
    left_in,
    right_in,
    map_in,
    map_bias,
    out,
    held,
    left_held,
    left_t,
    outer,
    map_rows,
    map_t,
    left_send,
    left_recv,
    ring_send,
    ring_recv,
    share_send,
    share_recv,
):
    chunks, count, chunk_lanes = held.shape
    lines = right_in.shape[0]
    left_lanes = left_held.shape[1]
    rows = out.shape[0]
    span = LANES
    width = chunk_lanes // span
    fold = LANES // width
    chips = ways // 2
    side_chips = chips // 2
    half_lanes = chunk_lanes // 2
    far = chips // 2

    me = lax.axis_index("row")
    core = lax.rem(me, 2)
    chip = me // 2
    level = chip // 2
    flank = lax.rem(chip, 2)
    place = level + flank * (chips - 1 - 2 * level)

    def device_at(position, kernel):
        turned = position // side_chips
        return 2 * (2 * position + turned * (2 * chips - 1 - 4 * position)) + kernel

    onward = (
        device_at(lax.rem(place + 1, chips), core),
        device_at(lax.rem(place + chips - 1, chips), core),
    )
    partner = me + 1 - 2 * core

    def origin(direction, hop):
        shift = chips - hop if direction == 0 else hop
        return lax.rem(place + shift, chips)

    def lines_of(device):
        return pl.ds(pl.multiple_of(device * lines, lines), lines)

    def ring(k, direction, half, hop, distance):
        ref = held.at[
            k,
            lines_of(device_at(origin(direction, distance), core)),
            pl.ds(half * half_lanes, half_lanes),
        ]
        return pltpu.make_async_remote_copy(
            src_ref=ref,
            dst_ref=ref,
            send_sem=ring_send.at[k, direction, half, hop - 1],
            recv_sem=ring_recv.at[k, direction, half, hop - 1],
            device_id={"row": onward[direction]},
            device_id_type=MESH,
        )

    def ring_start(k, direction, half, hop):
        ring(k, direction, half, hop, hop - 1).start()

    def ring_wait(k, direction, half, hop):
        ring(k, direction, half, hop, hop).wait_recv()

    def share(k, slot, kernel):
        direction = 0 if slot <= far else 1
        hop = slot if slot <= far else slot - far
        ref = held.at[k, lines_of(device_at(origin(direction, hop), kernel))]
        return pltpu.make_async_remote_copy(
            src_ref=ref,
            dst_ref=ref,
            send_sem=share_send.at[k, slot],
            recv_sem=share_recv.at[k, slot],
            device_id={"row": partner},
            device_id_type=MESH,
        )

    def begin(k):
        for half in range(2):
            for direction in range(2):
                ring_start(k, direction, half, 1)
        share(k, 0, core).start()

    def left_copy(step, target, source):
        return pltpu.make_async_remote_copy(
            src_ref=left_in.at[:, pl.ds(pl.multiple_of(target * left_lanes, left_lanes), left_lanes)],
            dst_ref=left_held.at[lines_of(source)],
            send_sem=left_send.at[step - 1],
            recv_sem=left_recv.at[step - 1],
            device_id={"row": target},
            device_id_type=MESH,
        )

    def outer_steps(k, first, last):
        @pl.loop(first, last)
        def _(step):
            part = jnp.dot(
                left_t[...],
                held[k, :, pl.ds(pl.multiple_of(step * (2 * span), 2 * span), 2 * span)],
                preferred_element_type=jnp.float32,
            )
            part = part.astype(jnp.bfloat16).reshape(rows // 2, 2, width, 2 * span)
            for half in range(2):
                spot = pl.ds(pl.multiple_of(step * (2 * width) + half * width, width), width)
                for side in range(2):
                    outer[:, spot, side * span : (side + 1) * span] = part[
                        :, side, :, half * span : (half + 1) * span
                    ]

    def map_steps(k, first, last):
        @pl.loop(first, last)
        def _(pair):
            mapped = jnp.dot(map_t[...], outer[pair], preferred_element_type=jnp.float32)
            mapped = mapped * (1.0 / count)
            for side in range(2):
                block = 2 * pair + side
                row = lax.rem(block, fold) * SUBLANES + block // fold
                out[row, pl.ds(pl.multiple_of(k * span, span), span), :] = (
                    mapped[:, side * span : (side + 1) * span].T + map_bias[...]
                ).astype(jnp.bfloat16)

    barrier = pltpu.get_barrier_semaphore()

    @pl.loop(1, ways)
    def _(step):
        pl.semaphore_signal(
            barrier, inc=1, device_id={"row": lax.rem(me + step, ways)}, device_id_type=MESH
        )

    for k in range(chunks):
        held[k, lines_of(me), :] = right_in[:, k * chunk_lanes : (k + 1) * chunk_lanes]
    pl.semaphore_wait(barrier, ways - 1)

    @pl.loop(1, ways)
    def _(step):
        left_copy(step, lax.rem(me + step, ways), me).start()

    begin(0)
    left_held[lines_of(me), :] = left_in[
        :, pl.ds(pl.multiple_of(me * left_lanes, left_lanes), left_lanes)
    ]

    quarter = width // 8
    third = rows // 2 // 4

    map_rows[...] = map_in[...].astype(jnp.float32)
    for at in range(0, width, fold):
        block = [map_rows[pl.ds(at + d, width, stride=width), :] for d in range(fold)]
        map_t[:, at * width : (at + fold) * width] = (
            jnp.concatenate(block, axis=0).T.astype(jnp.bfloat16)
        )

    begin(1)
    piece = width // 8

    @pl.loop(0, chunks + 2)
    def _(n):
        young = n < chunks
        old = jnp.logical_and(n >= 1, n <= chunks)
        ready = n >= 2

        def beside(*slices):
            @pl.when(ready)
            def _():
                for work, number in slices:
                    work(n - 2, number * piece, (number + 1) * piece)

        @pl.when(jnp.logical_and(n >= 1, n + 1 < chunks))
        def _():
            begin(n + 1)

        for half in range(2):

            @pl.when(old)
            def _():
                for direction in range(2):
                    ring_wait(n - 1, direction, half, far - 1)
                    if half == direction:
                        ring_start(n - 1, direction, half, far)

            @pl.when(young)
            def _():
                for direction in range(2):
                    ring_wait(n, direction, half, 1)
                    ring_start(n, direction, half, 2)

            beside((outer_steps, half))

        @pl.when(old)
        def _():
            share(n - 1, far - 1, core).start()
            share(n - 1, 2 * far - 1, core).start()

        @pl.when(young)
        def _():
            share(n, 1, core).start()
            share(n, far + 1, core).start()

        beside((outer_steps, 2))
        for half in range(2):

            @pl.when(young)
            def _():
                for direction in range(2):
                    ring_wait(n, direction, half, 2)
                    ring_start(n, direction, half, 3)

            beside((outer_steps, 3) if half == 0 else (map_steps, 0))

        @pl.when(young)
        def _():
            share(n, 2, core).start()
            share(n, far + 2, core).start()

        @pl.when(old)
        def _():
            ring_wait(n - 1, 0, 0, far)
            ring_wait(n - 1, 1, 1, far)
            share(n - 1, far, core).start()

        @pl.when(ready)
        def _():
            map_steps(n - 2, piece, rows // 2)

        @pl.when(old)
        def _():
            for slot in range(chips):
                share(n - 1, slot, 1 - core).wait_recv()

        @pl.when(n == 1)
        def _():
            @pl.loop(1, ways)
            def _(step):
                source = lax.rem(me + ways - step, ways)
                left_copy(step, lax.rem(me + step, ways), source).wait_recv()

            for at in range(0, left_lanes, 2 * LANES):
                left_t[at : at + 2 * LANES, :] = (
                    left_held[:, at : at + 2 * LANES].astype(jnp.float32).T.astype(jnp.bfloat16)
                )

    @pl.loop(1, ways)
    def _(step):
        left_copy(step, lax.rem(me + step, ways), me).wait_send()

    @pl.loop(0, chunks)
    def _(k):
        for direction in range(2):
            for half in range(2):
                for hop in range(1, far + 1):
                    if hop < far or half == direction:
                        ring(k, direction, half, hop, hop - 1).wait_send()
        for slot in range(chips):
            share(k, slot, core).wait_send()


def exchange_and_pair(left, right, final_map_kernel, final_map_bias, rows, ways):
    lines = right.shape[0]
    count = lines * ways
    pair_width = final_map_kernel.shape[1]
    cols = rows * ways
    width = right.shape[1] // cols
    chunks = cols // LANES
    chips = ways // 2
    whole = pl.BlockSpec(memory_space=pltpu.VMEM)
    return pl.pallas_call(
        functools.partial(fused_kernel, ways),
        in_specs=[whole] * 4,
        out_specs=whole,
        out_shape=jax.ShapeDtypeStruct((rows, cols, pair_width), jnp.bfloat16),
        scratch_shapes=[
            pltpu.VMEM((chunks, count, LANES * width), jnp.bfloat16),
            pltpu.VMEM((count, rows * width), jnp.bfloat16),
            pltpu.VMEM((rows * width, count), jnp.bfloat16),
            pltpu.VMEM((rows // 2, width * width, 2 * LANES), jnp.bfloat16),
            pltpu.VMEM((width * width, pair_width), jnp.float32),
            pltpu.VMEM((pair_width, width * width), jnp.bfloat16),
            pltpu.SemaphoreType.DMA((ways - 1,)),
            pltpu.SemaphoreType.DMA((ways - 1,)),
            pltpu.SemaphoreType.DMA((chunks, 2, 2, chips // 2)),
            pltpu.SemaphoreType.DMA((chunks, 2, 2, chips // 2)),
            pltpu.SemaphoreType.DMA((chunks, chips)),
            pltpu.SemaphoreType.DMA((chunks, chips)),
        ],
        compiler_params=pltpu.CompilerParams(
            collective_id=0, has_side_effects=True, vmem_limit_bytes=48 * 1024 * 1024
        ),
    )(
        left,
        right,
        final_map_kernel,
        final_map_bias.reshape(1, pair_width),
    )


def body(
    alignment_features,
    standardizer_gain,
    standardizer_shift,
    first_factor_kernel,
    first_factor_shift,
    second_factor_kernel,
    second_factor_shift,
    final_map_kernel,
    final_map_shift,
):
    left, right = project(
        alignment_features,
        standardizer_gain,
        standardizer_shift,
        first_factor_kernel,
        first_factor_shift,
        second_factor_kernel,
        second_factor_shift,
    )
    ways = lax.axis_size("row")
    rows = alignment_features.shape[1] // ways
    return exchange_and_pair(left, right, final_map_kernel, final_map_shift, rows, ways)


def plain_body(
    alignment_features,
    standardizer_gain,
    standardizer_shift,
    first_factor_kernel,
    first_factor_shift,
    second_factor_kernel,
    second_factor_shift,
    final_map_kernel,
    final_map_shift,
):
    width = first_factor_kernel.shape[1]
    arrived_lines = lax.all_to_all(
        alignment_features, "row", split_axis=1, concat_axis=0, tiled=True
    )
    left_flat, right_flat = project_flat(
        arrived_lines,
        standardizer_gain,
        standardizer_shift,
        first_factor_kernel,
        first_factor_shift,
        second_factor_kernel,
        second_factor_shift,
    )
    return pair_rows(
        left_flat,
        lax.all_gather(right_flat, "row", axis=1, tiled=True),
        width,
        final_map_kernel,
        final_map_shift,
    )


def solution(mesh):
    ways = mesh.shape["row"]
    groups = mesh.shape["groups"]

    def update(alignment_features, *parameters):
        total, residues, depth = alignment_features.shape
        width = parameters[2].shape[1]
        lines = total // (groups * ways)
        count = lines * ways
        fits = (
            ways == 16
            and lines % 16 == 0
            and count & (count - 1) == 0
            and width == 32
            and residues == 32 * ways
            and depth % LANES == 0
            and parameters[6].shape[1] == LANES
        )
        return jax.shard_map(
            body if fits else plain_body,
            mesh=mesh,
            in_specs=(P(("groups", "row"), None, None),) + (P(),) * len(parameters),
            out_specs=P(("groups", "row"), None, None),
            check_vma=False,
        )(alignment_features, *parameters)

    return update
```

```python
import functools

import jax
import jax.numpy as jnp
from jax import lax
from jax.experimental import pallas as pl
from jax.experimental.pallas import tpu as pltpu
from jax.sharding import PartitionSpec as P

LANES = 128
SUBLANES = 8


def largest_divisor(total, limit):
    return max((factor for factor in range(1, min(total, limit) + 1) if total % factor == 0))


def project_flat(
    block,
    standardizer_gain,
    standardizer_shift,
    first_factor_kernel,
    first_factor_shift,
    second_factor_kernel,
    second_factor_shift,
):
    incoming_features = block.astype(jnp.float32)
    center = incoming_features - jnp.mean(incoming_features, axis=-1, keepdims=True)
    spread = jnp.mean(center * center, axis=-1, keepdims=True)
    normed = (center * lax.rsqrt(spread + 1e-05) * standardizer_gain + standardizer_shift).astype(
        jnp.bfloat16
    )
    lines, residues = (normed.shape[0], normed.shape[1])
    first_mapped = jnp.einsum(
        "src,ck->srk", normed, first_factor_kernel, preferred_element_type=jnp.float32
    )
    second_mapped = jnp.einsum(
        "src,ck->srk", normed, second_factor_kernel, preferred_element_type=jnp.float32
    )
    first_flat = (first_mapped + first_factor_shift).astype(jnp.bfloat16).reshape(lines, -1)
    second_flat = (second_mapped + second_factor_shift).astype(jnp.bfloat16).reshape(lines, -1)
    return (first_flat, second_flat)


def pair_rows(left_flat, right_flat, width, final_map_kernel, final_map_shift):
    count = left_flat.shape[0]
    rows = left_flat.shape[1] // width
    cols = right_flat.shape[1] // width
    pair_width = final_map_kernel.shape[1]
    row_step = largest_divisor(rows, max(1, 2048 // cols))
    kernel_grid = final_map_kernel.reshape(width, width, pair_width)

    def one_block(index):
        left_part = lax.dynamic_slice_in_dim(
            left_flat, index * (row_step * width), row_step * width, 1
        )
        outer = lax.dot_general(
            left_part, right_flat, (((0,), (0,)), ((), ())), preferred_element_type=jnp.float32
        )
        outer = (outer / count).astype(jnp.bfloat16).reshape(row_step, width, cols, width)
        mapped = jnp.einsum("icjd,cdp->ijp", outer, kernel_grid, preferred_element_type=jnp.float32)
        return (mapped + final_map_shift).astype(jnp.bfloat16)

    blocks = lax.map(one_block, jnp.arange(rows // row_step, dtype=jnp.int32))
    return blocks.reshape(rows, cols, pair_width)


def project_kernel(
    features,
    gain,
    offset,
    first_t,
    first_bias,
    second_t,
    second_bias,
    left_out,
    right_out,
    first_spread,
    first_rows,
    second_rows,
):
    lines, span, depth = features.shape
    width = second_t.shape[0]
    fold = LANES // width
    owners = span // (fold * SUBLANES)

    @pl.when(pl.program_id(0) == 0)
    def _():
        first_spread[...] = jnp.zeros_like(first_spread)
        for m in range(fold):
            first_spread[m * width : (m + 1) * width, m * depth : (m + 1) * depth] = first_t[...]

    incoming = features[...].astype(jnp.float32).reshape(lines * span, depth)
    center = incoming - jnp.mean(incoming, axis=-1, keepdims=True)
    spread = jnp.mean(center * center, axis=-1, keepdims=True)
    normed = center * lax.rsqrt(spread + 1e-05) * gain[...] + offset[...]
    split = normed.reshape(lines * owners, fold, SUBLANES, depth)
    folded = jnp.concatenate(
        [split[:, m].reshape(lines * owners * SUBLANES, depth).astype(jnp.bfloat16) for m in range(fold)],
        axis=1,
    )
    first_rows[...] = (
        lax.dot_general(
            folded, first_spread[...], (((1,), (1,)), ((), ())), preferred_element_type=jnp.float32
        )
        + jnp.concatenate([first_bias[...]] * fold, axis=1)
    )
    flat = normed.astype(jnp.bfloat16)
    for s in range(lines):
        second_rows[s * width : (s + 1) * width, :] = lax.dot_general(
            second_t[...],
            flat[s * span : (s + 1) * span],
            (((1,), (1,)), ((), ())),
            preferred_element_type=jnp.float32,
        )
    per_line = owners * SUBLANES
    for q in range(per_line):
        left_out[:, q * LANES : (q + 1) * LANES] = first_rows[
            pl.ds(q, lines, stride=per_line), :
        ].astype(jnp.bfloat16)
    for d in range(width):
        right_out[:, d * span : (d + 1) * span] = (
            second_rows[pl.ds(d, lines, stride=width), :] + second_bias[d]
        ).astype(jnp.bfloat16)


def project(features, gain, offset, first_kernel, first_bias, second_kernel, second_bias):
    lines, residues, depth = features.shape
    width = first_kernel.shape[1]
    fold = LANES // width
    chunks = residues // LANES
    whole = pl.BlockSpec(memory_space=pltpu.VMEM)
    return pl.pallas_call(
        project_kernel,
        grid=(chunks,),
        in_specs=[pl.BlockSpec((lines, LANES, depth), lambda k: (0, k, 0))]
        + [whole] * 5
        + [pl.BlockSpec(memory_space=pltpu.SMEM)],
        out_specs=[
            pl.BlockSpec((lines, LANES * width), lambda k: (0, k)),
            pl.BlockSpec((lines, LANES * width), lambda k: (0, k)),
        ],
        out_shape=[jax.ShapeDtypeStruct((lines, residues * width), jnp.bfloat16)] * 2,
        scratch_shapes=[
            pltpu.VMEM((LANES, fold * depth), jnp.bfloat16),
            pltpu.VMEM((lines * LANES // fold, LANES), jnp.float32),
            pltpu.VMEM((lines * width, LANES), jnp.float32),
        ],
        compiler_params=pltpu.CompilerParams(vmem_limit_bytes=58 * 1024 * 1024),
    )(
        features,
        gain.reshape(1, depth),
        offset.reshape(1, depth),
        first_kernel.T,
        first_bias.reshape(1, width),
        second_kernel.T,
        second_bias,
    )


MESH = pl.DeviceIdType.MESH


def fused_kernel(
    ways,
    left_in,
    right_in,
    map_in,
    map_bias,
    out,
    held,
    left_held,
    left_t,
    outer,
    map_rows,
    map_t,
    left_send,
    left_recv,
    ring_send,
    ring_recv,
    share_send,
    share_recv,
):
    chunks, count, chunk_lanes = held.shape
    lines = right_in.shape[0]
    left_lanes = left_held.shape[1]
    rows = out.shape[0]
    span = LANES
    width = chunk_lanes // span
    fold = LANES // width
    chips = ways // 2
    side_chips = chips // 2
    half_lanes = chunk_lanes // 2
    far = chips // 2

    me = lax.axis_index("row")
    core = lax.rem(me, 2)
    chip = me // 2
    level = chip // 2
    flank = lax.rem(chip, 2)
    place = level + flank * (chips - 1 - 2 * level)

    def device_at(position, kernel):
        turned = position // side_chips
        return 2 * (2 * position + turned * (2 * chips - 1 - 4 * position)) + kernel

    onward = (
        device_at(lax.rem(place + 1, chips), core),
        device_at(lax.rem(place + chips - 1, chips), core),
    )
    partner = me + 1 - 2 * core

    def origin(direction, hop):
        shift = chips - hop if direction == 0 else hop
        return lax.rem(place + shift, chips)

    def lines_of(device):
        return pl.ds(pl.multiple_of(device * lines, lines), lines)

    def ring(k, direction, half, hop, distance):
        ref = held.at[
            k,
            lines_of(device_at(origin(direction, distance), core)),
            pl.ds(half * half_lanes, half_lanes),
        ]
        return pltpu.make_async_remote_copy(
            src_ref=ref,
            dst_ref=ref,
            send_sem=ring_send.at[k, direction, half, hop - 1],
            recv_sem=ring_recv.at[k, direction, half, hop - 1],
            device_id={"row": onward[direction]},
            device_id_type=MESH,
        )

    def ring_start(k, direction, half, hop):
        ring(k, direction, half, hop, hop - 1).start()

    def ring_wait(k, direction, half, hop):
        ring(k, direction, half, hop, hop).wait_recv()

    def share(k, slot, kernel):
        direction = 0 if slot <= far else 1
        hop = slot if slot <= far else slot - far
        ref = held.at[k, lines_of(device_at(origin(direction, hop), kernel))]
        return pltpu.make_async_remote_copy(
            src_ref=ref,
            dst_ref=ref,
            send_sem=share_send.at[k, slot],
            recv_sem=share_recv.at[k, slot],
            device_id={"row": partner},
            device_id_type=MESH,
        )

    def begin(k):
        for half in range(2):
            for direction in range(2):
                ring_start(k, direction, half, 1)
        share(k, 0, core).start()

    def left_copy(step, target, source):
        return pltpu.make_async_remote_copy(
            src_ref=left_in.at[:, pl.ds(pl.multiple_of(target * left_lanes, left_lanes), left_lanes)],
            dst_ref=left_held.at[lines_of(source)],
            send_sem=left_send.at[step - 1],
            recv_sem=left_recv.at[step - 1],
            device_id={"row": target},
            device_id_type=MESH,
        )

    def outer_steps(k, first, last):
        @pl.loop(first, last)
        def _(step):
            block = rows // 8
            for group in range(4):
                part = jnp.dot(
                    left_t[group * 2 * block * width : (group + 1) * 2 * block * width, :],
                    held[k, :, pl.ds(pl.multiple_of(step * (2 * span), 2 * span), 2 * span)],
                    preferred_element_type=jnp.float32,
                )
                part = part.astype(jnp.bfloat16).reshape(block, 2, width, 2 * span)
                for half in range(2):
                    spot = pl.ds(pl.multiple_of(step * (2 * width) + half * width, width), width)
                    for side in range(2):
                        outer[
                            group * block : (group + 1) * block,
                            spot,
                            side * span : (side + 1) * span,
                        ] = part[:, side, :, half * span : (half + 1) * span]

    def map_steps(k, first, last):
        @pl.loop(first, last, unroll=4)
        def _(pair):
            mapped = jnp.dot(map_t[...], outer[pair], preferred_element_type=jnp.float32)
            mapped = mapped * (1.0 / count)
            for side in range(2):
                block = 2 * pair + side
                row = lax.rem(block, fold) * SUBLANES + block // fold
                out[row, pl.ds(pl.multiple_of(k * span, span), span), :] = (
                    mapped[:, side * span : (side + 1) * span].T + map_bias[...]
                ).astype(jnp.bfloat16)

    barrier = pltpu.get_barrier_semaphore()

    @pl.loop(1, ways)
    def _(step):
        pl.semaphore_signal(
            barrier, inc=1, device_id={"row": lax.rem(me + step, ways)}, device_id_type=MESH
        )

    for k in range(chunks):
        held[k, lines_of(me), :] = right_in[:, k * chunk_lanes : (k + 1) * chunk_lanes]
    pl.semaphore_wait(barrier, ways - 1)

    @pl.loop(1, ways)
    def _(step):
        left_copy(step, lax.rem(me + step, ways), me).start()

    begin(0)
    left_held[lines_of(me), :] = left_in[
        :, pl.ds(pl.multiple_of(me * left_lanes, left_lanes), left_lanes)
    ]

    quarter = width // 8
    third = rows // 2 // 4

    map_rows[...] = map_in[...].astype(jnp.float32)
    for at in range(0, width, fold):
        block = [map_rows[pl.ds(at + d, width, stride=width), :] for d in range(fold)]
        map_t[:, at * width : (at + fold) * width] = (
            jnp.concatenate(block, axis=0).T.astype(jnp.bfloat16)
        )

    begin(1)
    piece = width // 8

    @pl.loop(0, chunks + 2)
    def _(n):
        young = n < chunks
        old = jnp.logical_and(n >= 1, n <= chunks)
        ready = n >= 2

        def beside(*slices):
            @pl.when(ready)
            def _():
                for work, number in slices:
                    work(n - 2, number * piece, (number + 1) * piece)

        @pl.when(jnp.logical_and(n >= 1, n + 1 < chunks))
        def _():
            begin(n + 1)

        for half in range(2):

            @pl.when(old)
            def _():
                for direction in range(2):
                    ring_wait(n - 1, direction, half, far - 1)
                    if half == direction:
                        ring_start(n - 1, direction, half, far)

            @pl.when(young)
            def _():
                for direction in range(2):
                    ring_wait(n, direction, half, 1)
                    ring_start(n, direction, half, 2)

            beside((outer_steps, half))

        @pl.when(old)
        def _():
            share(n - 1, far - 1, core).start()
            share(n - 1, 2 * far - 1, core).start()

        @pl.when(young)
        def _():
            share(n, 1, core).start()
            share(n, far + 1, core).start()

        beside((outer_steps, 2))
        for half in range(2):

            @pl.when(young)
            def _():
                for direction in range(2):
                    ring_wait(n, direction, half, 2)
                    ring_start(n, direction, half, 3)

            beside((outer_steps, 3) if half == 0 else (map_steps, 0))

        @pl.when(young)
        def _():
            share(n, 2, core).start()
            share(n, far + 2, core).start()

        @pl.when(old)
        def _():
            ring_wait(n - 1, 0, 0, far)
            ring_wait(n - 1, 1, 1, far)
            share(n - 1, far, core).start()

        @pl.when(ready)
        def _():
            map_steps(n - 2, piece, rows // 2)

        @pl.when(old)
        def _():
            for slot in range(chips):
                share(n - 1, slot, 1 - core).wait_recv()

        @pl.when(n == 1)
        def _():
            @pl.loop(1, ways)
            def _(step):
                source = lax.rem(me + ways - step, ways)
                left_copy(step, lax.rem(me + step, ways), source).wait_recv()

            for at in range(0, left_lanes, 2 * LANES):
                left_t[at : at + 2 * LANES, :] = (
                    left_held[:, at : at + 2 * LANES].astype(jnp.float32).T.astype(jnp.bfloat16)
                )

    @pl.loop(1, ways)
    def _(step):
        left_copy(step, lax.rem(me + step, ways), me).wait_send()

    @pl.loop(0, chunks)
    def _(k):
        for direction in range(2):
            for half in range(2):
                for hop in range(1, far + 1):
                    if hop < far or half == direction:
                        ring(k, direction, half, hop, hop - 1).wait_send()
        for slot in range(chips):
            share(k, slot, core).wait_send()


def exchange_and_pair(left, right, final_map_kernel, final_map_bias, rows, ways):
    lines = right.shape[0]
    count = lines * ways
    pair_width = final_map_kernel.shape[1]
    cols = rows * ways
    width = right.shape[1] // cols
    chunks = cols // LANES
    chips = ways // 2
    whole = pl.BlockSpec(memory_space=pltpu.VMEM)
    return pl.pallas_call(
        functools.partial(fused_kernel, ways),
        in_specs=[whole] * 4,
        out_specs=whole,
        out_shape=jax.ShapeDtypeStruct((rows, cols, pair_width), jnp.bfloat16),
        scratch_shapes=[
            pltpu.VMEM((chunks, count, LANES * width), jnp.bfloat16),
            pltpu.VMEM((count, rows * width), jnp.bfloat16),
            pltpu.VMEM((rows * width, count), jnp.bfloat16),
            pltpu.VMEM((rows // 2, width * width, 2 * LANES), jnp.bfloat16),
            pltpu.VMEM((width * width, pair_width), jnp.float32),
            pltpu.VMEM((pair_width, width * width), jnp.bfloat16),
            pltpu.SemaphoreType.DMA((ways - 1,)),
            pltpu.SemaphoreType.DMA((ways - 1,)),
            pltpu.SemaphoreType.DMA((chunks, 2, 2, chips // 2)),
            pltpu.SemaphoreType.DMA((chunks, 2, 2, chips // 2)),
            pltpu.SemaphoreType.DMA((chunks, chips)),
            pltpu.SemaphoreType.DMA((chunks, chips)),
        ],
        compiler_params=pltpu.CompilerParams(
            collective_id=0, has_side_effects=True, vmem_limit_bytes=48 * 1024 * 1024
        ),
    )(
        left,
        right,
        final_map_kernel,
        final_map_bias.reshape(1, pair_width),
    )


def body(
    alignment_features,
    standardizer_gain,
    standardizer_shift,
    first_factor_kernel,
    first_factor_shift,
    second_factor_kernel,
    second_factor_shift,
    final_map_kernel,
    final_map_shift,
):
    left, right = project(
        alignment_features,
        standardizer_gain,
        standardizer_shift,
        first_factor_kernel,
        first_factor_shift,
        second_factor_kernel,
        second_factor_shift,
    )
    ways = lax.axis_size("row")
    rows = alignment_features.shape[1] // ways
    return exchange_and_pair(left, right, final_map_kernel, final_map_shift, rows, ways)


def plain_body(
    alignment_features,
    standardizer_gain,
    standardizer_shift,
    first_factor_kernel,
    first_factor_shift,
    second_factor_kernel,
    second_factor_shift,
    final_map_kernel,
    final_map_shift,
):
    width = first_factor_kernel.shape[1]
    arrived_lines = lax.all_to_all(
        alignment_features, "row", split_axis=1, concat_axis=0, tiled=True
    )
    left_flat, right_flat = project_flat(
        arrived_lines,
        standardizer_gain,
        standardizer_shift,
        first_factor_kernel,
        first_factor_shift,
        second_factor_kernel,
        second_factor_shift,
    )
    return pair_rows(
        left_flat,
        lax.all_gather(right_flat, "row", axis=1, tiled=True),
        width,
        final_map_kernel,
        final_map_shift,
    )


def solution(mesh):
    ways = mesh.shape["row"]
    groups = mesh.shape["groups"]

    def update(alignment_features, *parameters):
        total, residues, depth = alignment_features.shape
        width = parameters[2].shape[1]
        lines = total // (groups * ways)
        count = lines * ways
        fits = (
            ways == 16
            and lines % 16 == 0
            and count & (count - 1) == 0
            and width == 32
            and residues == 32 * ways
            and depth % LANES == 0
            and parameters[6].shape[1] == LANES
        )
        return jax.shard_map(
            body if fits else plain_body,
            mesh=mesh,
            in_specs=(P(("groups", "row"), None, None),) + (P(),) * len(parameters),
            out_specs=P(("groups", "row"), None, None),
            check_vma=False,
        )(alignment_features, *parameters)

    return update
```
